32 devices in a mesh: seq: 8 (over y, x, core), tensor: 4 (over z).
Axes of the slice: x: 2, y: 2, z: 4, core: 2. Of those that a mesh axis runs over, the one named last changes fastest.
Arguments:
- out_grad: bfloat16 [1024, 4096], P('seq', 'tensor'), may hold values from -3 to 3
- down_weight: bfloat16 [8, 256, 4096], P('tensor'), may hold values from -0.09375 to 0.09375
- pre_act: bfloat16 [8, 8, 128, 512], P('seq', 'tensor'), may hold values from -6 to 6
- gate_prob: float32 [8, 8, 128], P('seq', 'tensor'), may hold values from 0.1 to 1
- slot_token: int32 [8, 8, 128], P('seq', 'tensor'), may hold values from 0 to 127, as said below
- slot_count: int32 [8, 8], P('seq', 'tensor'), may hold values from 16 to 128, as said below
Outputs:
- pre_grad: bfloat16 [8, 8, 128, 512], P('seq', 'tensor')
- prob_grad: float32 [8, 8, 128], P('seq', 'tensor')
- weight_grad: bfloat16 [8, 256, 4096], P('tensor', None, 'seq')
The draws below stay inside these ranges and needn't reach their ends.
Inputs may be any that keep to these rules, and one draw needn't show every extreme that they name: `slot_token`: for each group and expert the 128 slots list every token of the group once; slots from slot_count on hold tokens too and are not live. `slot_count`: some expert of some group has all 128 slots live.
All inputs are finite; a program needn't handle non-finite values.
Results may differ from the reference program's by a relative error of at most 0.015.
Values may be sent and summed in bfloat16 or wider, within the bound.
A program may use at most 64 MiB of HBM per device.

```python
import math
import jax
import jax.numpy as jnp
from jax import lax

D = 4096
H = 256
EXPERTS = 8
TOK_DEV = 128
TOKENS = 1024
N_SEQ = 8


def draw_slot_token(key, part):
    key = jax.random.fold_in(key, 11)
    keys = jax.random.split(key, N_SEQ * EXPERTS)
    orders = jax.vmap(lambda single: jax.random.permutation(single, TOK_DEV))(keys)
    return orders.reshape(N_SEQ, EXPERTS, TOK_DEV).astype(jnp.int32)


def draw_slot_count(key, part):
    key = jax.random.fold_in(key, 23)
    first, fourth = jax.random.split(key, 2)
    shape = (N_SEQ * EXPERTS,)
    counts = jax.random.randint(first, shape, TOK_DEV // 8, TOK_DEV + 1)
    chosen = jax.random.randint(fourth, (), 0, N_SEQ * EXPERTS)
    places = jnp.arange(N_SEQ * EXPERTS, dtype=jnp.int32)
    counts = jnp.where(places == chosen, TOK_DEV, counts)
    return counts.reshape(N_SEQ, EXPERTS).astype(jnp.int32)


def raised(entries, rng, source, target, blocks, factor):
    owner, partner = [(jnp.arange(entries.shape[dim]) // (entries.shape[dim] // blocks)).reshape([-1 if axis == dim else 1 for axis in range(entries.ndim)]) for dim in (source, target)]
    chosen = jax.random.permutation(rng, blocks)[partner]
    strong = (owner == chosen) | (owner == (partner + blocks // 2) % blocks)
    return jnp.where(strong, factor * entries, entries)


def steps_of(own_key, dims, pieces, smallest, largest):
    def one(axis_at, parts):
        heights = jax.random.uniform(jax.random.fold_in(jax.random.fold_in(own_key, 6), axis_at), (parts,), jnp.float32, smallest / len(pieces), largest / len(pieces))
        return jnp.repeat(jnp.exp(heights), dims[axis_at] // parts).reshape((-1,) + (1,) * (len(dims) - axis_at - 1))

    gain = one(*pieces[0])
    for cut in pieces[1:]:
        gain = gain * one(*cut)
    return gain


def bell_draw(key, shape, scale, reach, cuts=(), kind=jnp.bfloat16):
    drawn = scale * jax.random.normal(key, shape, jnp.float32)
    if cuts:
        drawn = drawn * steps_of(key, shape, cuts, -0.22, 0.18)
    return jnp.clip(drawn, -reach, reach).astype(kind)


def heavy_noise(key, shape, deviation, most, cuts, heavy, kind=jnp.bfloat16):
    entries = deviation * jax.random.normal(key, shape, jnp.float32)
    if cuts:
        entries = entries * steps_of(key, shape, cuts, -0.22, 0.18)
    return jnp.clip(raised(entries, jax.random.fold_in(key, 3), *heavy), -most, most).astype(kind)


def setup_inputs(seed: int = 0) -> dict:
    key_list = jax.random.split(jax.random.key(seed), 7)
    out_grad = heavy_noise(key_list[0], (TOKENS, D), 0.5, 3.0, ((0, 8), (1, 4)), (0, 1, 8, 2.0))
    down_weight = bell_draw(key_list[1], (EXPERTS, H, D), D ** -0.5, 0.09375, ((0, 4),))
    pre_act = bell_draw(key_list[2], (N_SEQ, EXPERTS, TOK_DEV, 2 * H), 1.0, 6.0, ((0, 8), (1, 4)))
    gate_prob = jnp.clip(jnp.exp(math.log(1.0) - 2.3025851 * jax.random.uniform(key_list[3], (N_SEQ, EXPERTS, TOK_DEV), jnp.float32) ** steps_of(key_list[3], (N_SEQ, EXPERTS, TOK_DEV), ((0, 8), (1, 4)), -0.2, 0.2)), 0.1, 1.0)
    slot_token = draw_slot_token(jax.random.fold_in(key_list[6], 71), 0)
    slot_count = draw_slot_count(jax.random.fold_in(key_list[6], 71), 0)
    return dict(out_grad=out_grad, down_weight=down_weight, pre_act=pre_act, gate_prob=gate_prob, slot_token=slot_token, slot_count=slot_count)


def expert_block(token_rows, pre_block, gate_probs, live_mask, expert_weight):
    width = expert_weight.shape[0]
    gate_val = pre_block[:, :width].astype(jnp.float32)
    up_val = pre_block[:, width:].astype(jnp.float32)
    sigma_gate = jax.nn.sigmoid(gate_val)
    silu_gate = gate_val * sigma_gate
    activation = (silu_gate * up_val).astype(jnp.bfloat16)
    raw_grad = lax.dot_general(token_rows, expert_weight, (((1,), (1,)), ((), ())), preferred_element_type=jnp.float32)
    prob_grad = jnp.where(live_mask, jnp.sum(activation.astype(jnp.float32) * raw_grad, axis=1), 0.0)
    hidden_grad = gate_probs[:, None] * raw_grad
    gate_grad = hidden_grad * up_val * sigma_gate * (1.0 + gate_val * (1.0 - sigma_gate))
    up_grad = hidden_grad * silu_gate
    pre_grad = jnp.where(live_mask[:, None], jnp.concatenate([gate_grad, up_grad], axis=1), 0.0).astype(jnp.bfloat16)
    weighted = jnp.where(live_mask[:, None], gate_probs[:, None] * activation.astype(jnp.float32), 0.0).astype(jnp.bfloat16)
    weight_term = lax.dot_general(weighted, token_rows, (((0,), (0,)), ((), ())), preferred_element_type=jnp.float32)
    return pre_grad, prob_grad, weight_term


def reference(out_grad, down_weight, pre_act, gate_prob, slot_token, slot_count):
    grouped = out_grad.reshape(N_SEQ, TOK_DEV, D)
    positions = jnp.arange(TOK_DEV, dtype=jnp.int32)

    def per_expert(inputs):
        expert_weight, pre_all, prob_all, token_all, count_all = inputs

        def per_group(total, group_inputs):
            group_grads, pre_block, gate_probs, tokens, live_count = group_inputs
            token_rows = jnp.take(group_grads, tokens.astype(jnp.int32), axis=0)
            live_mask = positions < live_count
            pre_grad, prob_grad, weight_term = expert_block(token_rows, pre_block, gate_probs, live_mask, expert_weight)
            rounded = lax.optimization_barrier(weight_term.astype(jnp.bfloat16))
            return total + rounded.astype(jnp.float32), (pre_grad, prob_grad)

        start_total = jnp.zeros((H, D), jnp.float32)
        total, (pre_grads, prob_grads) = lax.scan(per_group, start_total, (grouped, pre_all, prob_all, token_all, count_all))
        return pre_grads, prob_grads, total.astype(jnp.bfloat16)

    pre_grads, prob_grads, weight_grad = lax.map(per_expert, (down_weight, jnp.swapaxes(pre_act, 0, 1), jnp.swapaxes(gate_prob, 0, 1), jnp.swapaxes(slot_token, 0, 1), jnp.swapaxes(slot_count, 0, 1)))
    return jnp.swapaxes(pre_grads, 0, 1), jnp.swapaxes(prob_grads, 0, 1), weight_grad
```

```python
import functools

import jax
import jax.numpy as jnp
from jax import lax
from jax.experimental import pallas as pl
from jax.experimental.pallas import tpu as pltpu
from jax.sharding import PartitionSpec as P

MESH = pl.DeviceIdType.MESH
PIECES = 2
AHEAD = 1


def token_slots(tok_ref, count_ref, expert, tokens):
    token = lax.broadcasted_iota(jnp.int32, (tokens, tokens), 0)
    slot = lax.broadcasted_iota(jnp.int32, (tokens, tokens), 1)
    hot = token == tok_ref[0, expert : expert + 1, :]
    return hot, hot & (slot < count_ref[0, expert])


def kernel(
    n_seq, n_tensor,
    count_ref, tok_ref, prob_ref, grad_ref, weight_ref, pre_ref,
    pre_out, prob_out, weight_out,
    rows, cols, scaled, weight, pre, coef, act, raw, total,
    local_sem, z_send, z_recv, c_send, c_recv, w_send, w_recv, f_send,
):
    s = lax.axis_index("seq")
    t = lax.axis_index("tensor")
    experts, hidden, _ = weight_ref.shape
    tokens = grad_ref.shape[0]
    block = cols.shape[1]
    halves = n_seq // n_tensor
    part = tokens // PIECES
    rounds = [(q, k) for q in range(PIECES) for k in range(halves)]
    sibling = s + 1 - 2 * lax.rem(s, 2)

    barrier = pltpu.get_barrier_semaphore()
    for i in range(1, n_seq):
        pl.semaphore_signal(barrier, inc=1, device_id=(lax.rem(s + i, n_seq), t), device_id_type=MESH)

    @pl.when(t > 0)
    def _():
        pl.semaphore_signal(barrier, inc=1, device_id=(s, t - 1), device_id_type=MESH)

    @pl.when(t < n_tensor - 1)
    def _():
        pl.semaphore_signal(barrier, inc=1, device_id=(s, t + 1), device_id_type=MESH)

    pre_copy = pltpu.make_async_copy(pre_ref.at[0], pre, local_sem.at[0])
    pre_copy.start()
    own_copies = []
    for k in range(halves):
        own_copies.append(
            pltpu.make_async_copy(
                grad_ref.at[:, pl.ds(k * block, block)], rows.at[t, k], local_sem.at[2 + k]
            )
        )
        own_copies[-1].start()
    weight_copy = pltpu.make_async_copy(weight_ref, weight, local_sem.at[1])
    weight_copy.start()
    pl.semaphore_wait(barrier, n_seq - 1 + (t > 0).astype(jnp.int32) + (t < n_tensor - 1).astype(jnp.int32))

    def piece(shard, q, k):
        return rows.at[shard, k, pl.ds(q * part, part), :]

    def source(shard, q, k, own):
        if own:
            return grad_ref.at[pl.ds(q * part, part), pl.ds(k * block, block)]
        return piece(shard, q, k)

    def z_copy(shard, q, k, way, own):
        p = q * halves + k
        return pltpu.make_async_remote_copy(
            src_ref=source(shard, q, k, own),
            dst_ref=piece(shard, q, k),
            send_sem=z_send.at[way, shard, p],
            recv_sem=z_recv.at[shard, p],
            device_id=(s, t + 1 if way == 0 else t - 1),
            device_id_type=MESH,
        )

    def c_copy(shard, q, k, own):
        return pltpu.make_async_remote_copy(
            src_ref=source(shard, q, k, own),
            dst_ref=cols.at[pl.ds(pl.multiple_of(s * tokens + q * part, part), part), :],
            send_sem=c_send.at[shard, q * halves + k],
            recv_sem=c_recv.at[s, q],
            device_id=(shard * halves + k, t),
            device_id_type=MESH,
        )

    def z_go(shard, q, k, way, own):
        @pl.when(t < n_tensor - 1 if way == 0 else t > 0)
        def _():
            z_copy(shard, q, k, way, own).start()

    def c_go(shard, q, k, own):
        @pl.when(shard * halves + k != s)
        def _():
            c_copy(shard, q, k, own).start()

    def w_copy(i):
        return pltpu.make_async_remote_copy(
            src_ref=scaled.at[pl.ds(pl.multiple_of(s * tokens, tokens), tokens), :],
            dst_ref=scaled.at[pl.ds(pl.multiple_of(s * tokens, tokens), tokens), :],
            send_sem=w_send.at[i],
            recv_sem=w_recv.at[s],
            device_id=(sibling if i == 0 else lax.rem(s + 2 * i, n_seq), t),
            device_id_type=MESH,
        )

    def f_copy(i):
        origin = lax.rem(s + n_seq - 2 * i, n_seq)
        at = scaled.at[pl.ds(pl.multiple_of(origin * tokens, tokens), tokens), :]
        return pltpu.make_async_remote_copy(
            src_ref=at, dst_ref=at, send_sem=f_send.at[i], recv_sem=w_recv.at[origin],
            device_id=(sibling, t), device_id_type=MESH,
        )

    def multiply(shard, q, k):
        left = rows[shard, k, q * part : (q + 1) * part, :]
        at = pl.ds(pl.multiple_of((shard * halves + k) * block, block), block)
        for e in range(experts):
            raw[q * part : (q + 1) * part, e * hidden : (e + 1) * hidden] += lax.dot_general(
                left, weight[e, :, at], (((1,), (1,)), ((), ())), preferred_element_type=jnp.float32
            )

    def send_own(p):
        q, k = rounds[p]
        z_go(t, q, k, 0, True)
        z_go(t, q, k, 1, True)
        c_go(t, q, k, True)

    for p in range(min(AHEAD + 1, len(rounds))):
        send_own(p)

    pre_copy.wait()
    for e in range(experts):
        hot, live = token_slots(tok_ref, count_ref, e, tokens)
        ordered = jnp.dot(hot.astype(jnp.bfloat16), pre[e], preferred_element_type=jnp.float32)
        probs = jnp.sum(jnp.where(live, prob_ref[0, e : e + 1, :], 0.0), axis=1, keepdims=True)
        gate, up = ordered[:, :hidden], ordered[:, hidden:]
        sigma = jax.nn.sigmoid(gate)
        silu = gate * sigma
        active = (silu * up).astype(jnp.bfloat16)
        act[:, e * hidden : (e + 1) * hidden] = active
        scaled[pl.ds(pl.multiple_of(s * tokens, tokens), tokens), e * hidden : (e + 1) * hidden] = (
            probs * active.astype(jnp.float32)
        ).astype(jnp.bfloat16)
        coef[e, :, :hidden] = probs * up * sigma * (1.0 + gate * (1.0 - sigma))
        coef[e, :, hidden:] = probs * silu
    for i in range(1, n_seq // 2):
        w_copy(i).start()
    w_copy(0).start()
    raw[...] = jnp.zeros_like(raw)
    for copy in own_copies:
        copy.wait()
    weight_copy.wait()

    def add_groups(q, first):
        for g in range(n_seq):
            at = pl.ds(g * tokens + q * part, part)
            term = lax.dot_general(
                scaled[at, :], cols[at, :], (((0,), (0,)), ((), ())), preferred_element_type=jnp.float32
            )
            if first and g == 0:
                total[...] = term
            else:
                total[...] += term

    def wait_groups(q):
        for g in range(n_seq):
            @pl.when(g != s)
            def _():
                at = cols.at[pl.ds(g * tokens + q * part, part), :]
                pltpu.make_async_remote_copy(
                    src_ref=at, dst_ref=at, send_sem=c_send.at[0, 0], recv_sem=c_recv.at[g, q],
                    device_id=(sibling, t), device_id_type=MESH,
                ).wait_recv()

    def use(shard, q, k):
        c_go(shard, q, k, False)
        multiply(shard, q, k)

    for p, (q, k) in enumerate(rounds):
        if p > 0 and p + AHEAD < len(rounds):
            send_own(p + AHEAD)
        for d in range(1, n_tensor):
            @pl.when(t >= d)
            def _():
                z_copy(t - d, q, k, 1, False).wait_recv()
                z_go(t - d, q, k, 0, False)
                use(t - d, q, k)

            @pl.when(t + d < n_tensor)
            def _():
                z_copy(t + d, q, k, 0, False).wait_recv()
                z_go(t + d, q, k, 1, False)
                use(t + d, q, k)
        multiply(t, q, k)
        if p == min(1, len(rounds) - 1):
            for i in range(1, n_seq // 2):
                f_copy(i).wait_recv()
                f_copy(i).start()

    cols[pl.ds(pl.multiple_of(s * tokens, tokens), tokens), :] = rows[lax.div(s, halves), lax.rem(s, halves)]
    for e in range(experts):
        hot, live = token_slots(tok_ref, count_ref, e, tokens)
        part_raw = raw[:, e * hidden : (e + 1) * hidden]
        grads = jnp.concatenate(
            [coef[e, :, :hidden] * part_raw, coef[e, :, hidden:] * part_raw], axis=1
        ).astype(jnp.bfloat16)
        pre_out[0, e] = lax.dot_general(
            hot.astype(jnp.bfloat16), grads, (((0,), (0,)), ((), ())), preferred_element_type=jnp.float32
        ).astype(jnp.bfloat16)
        sums = jnp.sum(
            act[:, e * hidden : (e + 1) * hidden].astype(jnp.float32) * part_raw, axis=1, keepdims=True
        )
        prob_out[0, e : e + 1, :] = jnp.sum(jnp.where(live, sums, 0.0), axis=0, keepdims=True)

    for g in range(n_seq):
        @pl.when(lax.rem(g, 2) != lax.rem(s, 2))
        def _():
            at = scaled.at[pl.ds(g * tokens, tokens), :]
            pltpu.make_async_remote_copy(
                src_ref=at, dst_ref=at, send_sem=w_send.at[0], recv_sem=w_recv.at[g],
                device_id=(sibling, t), device_id_type=MESH,
            ).wait_recv()
    for q in range(PIECES):
        wait_groups(q)
        add_groups(q, q == 0)
    for e in range(experts):
        weight_out[e] = total[e * hidden : (e + 1) * hidden, :].astype(jnp.bfloat16)

    for i in range(n_seq // 2):
        w_copy(i).wait_send()
    for i in range(1, n_seq // 2):
        f_copy(i).wait_send()
    for shard in range(n_tensor):
        for q, k in rounds:
            @pl.when(shard * halves + k != s)
            def _():
                c_copy(shard, q, k, False).wait_send()

            @pl.when((shard <= t) & (t < n_tensor - 1))
            def _():
                z_copy(shard, q, k, 0, False).wait_send()

            @pl.when((shard >= t) & (t > 0))
            def _():
                z_copy(shard, q, k, 1, False).wait_send()


def per_device(n_seq, n_tensor, out_grad, down_weight, pre_act, gate_prob, slot_token, slot_count):
    tokens, shard = out_grad.shape
    experts, hidden, width = down_weight.shape
    block = width // n_seq
    halves = n_seq // n_tensor
    pieces = PIECES * halves
    whole = pl.BlockSpec(memory_space=pltpu.VMEM)
    away = pl.BlockSpec(memory_space=pl.ANY)
    dma = pltpu.SemaphoreType.DMA
    return pl.pallas_call(
        functools.partial(kernel, n_seq, n_tensor),
        out_shape=(
            jax.ShapeDtypeStruct((1, experts, tokens, 2 * hidden), jnp.bfloat16),
            jax.ShapeDtypeStruct((1, experts, tokens), jnp.float32),
            jax.ShapeDtypeStruct((experts, hidden, block), jnp.bfloat16),
        ),
        in_specs=[pl.BlockSpec(memory_space=pltpu.SMEM), whole, whole, away, away, away],
        out_specs=(whole, whole, whole),
        scratch_shapes=[
            pltpu.VMEM((n_tensor, halves, tokens, block), jnp.bfloat16),
            pltpu.VMEM((n_seq * tokens, block), jnp.bfloat16),
            pltpu.VMEM((n_seq * tokens, experts * hidden), jnp.bfloat16),
            pltpu.VMEM((experts, hidden, width), jnp.bfloat16),
            pltpu.VMEM((experts, tokens, 2 * hidden), jnp.bfloat16),
            pltpu.VMEM((experts, tokens, 2 * hidden), jnp.float32),
            pltpu.VMEM((tokens, experts * hidden), jnp.bfloat16),
            pltpu.VMEM((tokens, experts * hidden), jnp.float32),
            pltpu.VMEM((experts * hidden, block), jnp.float32),
            dma((2 + halves,)),
            dma((2, n_tensor, pieces)),
            dma((n_tensor, pieces)),
            dma((n_tensor, pieces)),
            dma((n_seq, PIECES)),
            dma((n_seq // 2,)),
            dma((n_seq,)),
            dma((n_seq // 2,)),
        ],
        compiler_params=pltpu.CompilerParams(
            collective_id=0, has_side_effects=True, vmem_limit_bytes=40 * 1024 * 1024
        ),
    )(slot_count, slot_token, gate_prob, out_grad, down_weight, pre_act)


def solution(mesh):
    placed = (
        P("seq", "tensor"),
        P("tensor", None, None),
        P("seq", "tensor", None, None),
        P("seq", "tensor", None),
        P("seq", "tensor", None),
        P("seq", "tensor"),
    )
    return jax.shard_map(
        functools.partial(per_device, mesh.shape["seq"], mesh.shape["tensor"]),
        mesh=mesh,
        in_specs=placed,
        out_specs=(
            P("seq", "tensor", None, None),
            P("seq", "tensor", None),
            P("tensor", None, "seq"),
        ),
        check_vma=False,
    )
```

```python
import functools

import jax
import jax.numpy as jnp
from jax import lax
from jax.experimental import pallas as pl
from jax.experimental.pallas import tpu as pltpu
from jax.sharding import PartitionSpec as P

MESH = pl.DeviceIdType.MESH
PIECES = 2
AHEAD = 1
DIRECT = 2


def token_slots(tok_ref, count_ref, expert, tokens):
    token = lax.broadcasted_iota(jnp.int32, (tokens, tokens), 0)
    slot = lax.broadcasted_iota(jnp.int32, (tokens, tokens), 1)
    hot = token == tok_ref[expert : expert + 1, :]
    return hot, hot & (slot < count_ref[0, expert])


def kernel(
    n_seq, n_tensor,
    count_in, tok_in, prob_in, grad_ref, weight_ref, pre_ref,
    pre_out, prob_out, weight_out,
    count_ref, tok_ref, prob_ref, rows, cols, scaled, weight, pre, coef, act, raw, total,
    local_sem, o_send, z_send, z_recv, c_send, c_recv, w_send, w_recv, f_send,
):
    s = lax.axis_index("seq")
    t = lax.axis_index("tensor")
    experts, hidden, _ = weight_ref.shape
    tokens = grad_ref.shape[0]
    block = cols.shape[1]
    halves = n_seq // n_tensor
    part = tokens // PIECES
    reach = min(DIRECT, n_tensor - 1)
    rounds = [(q, k) for q in range(PIECES) for k in range(halves)]
    sibling = s + 1 - 2 * lax.rem(s, 2)

    barrier = pltpu.get_barrier_semaphore()
    for i in range(1, n_seq):
        pl.semaphore_signal(barrier, inc=1, device_id=(lax.rem(s + i, n_seq), t), device_id_type=MESH)

    greeted = n_seq - 1
    for steps in range(1, reach + 1):
        @pl.when(t >= steps)
        def _():
            pl.semaphore_signal(barrier, inc=1, device_id=(s, t - steps), device_id_type=MESH)

        @pl.when(t + steps < n_tensor)
        def _():
            pl.semaphore_signal(barrier, inc=1, device_id=(s, t + steps), device_id_type=MESH)

        greeted += (t >= steps).astype(jnp.int32) + (t + steps < n_tensor).astype(jnp.int32)

    first_copies = [
        pltpu.make_async_copy(pre_ref.at[0], pre, local_sem.at[0]),
        pltpu.make_async_copy(count_in, count_ref, local_sem.at[1]),
        pltpu.make_async_copy(tok_in.at[0], tok_ref, local_sem.at[2]),
        pltpu.make_async_copy(prob_in.at[0], prob_ref, local_sem.at[3]),
    ]
    for copy in first_copies:
        copy.start()
    own_copies = []
    for k in range(halves):
        own_copies.append(
            pltpu.make_async_copy(
                grad_ref.at[:, pl.ds(k * block, block)], rows.at[t, k], local_sem.at[5 + k]
            )
        )
        own_copies[-1].start()
    weight_copy = pltpu.make_async_copy(weight_ref, weight, local_sem.at[4])
    weight_copy.start()
    pl.semaphore_wait(barrier, greeted)

    def piece(shard, q, k):
        return rows.at[shard, k, pl.ds(q * part, part), :]

    def source(shard, q, k, own):
        if own:
            return grad_ref.at[pl.ds(q * part, part), pl.ds(k * block, block)]
        return piece(shard, q, k)

    def z_copy(shard, q, k, way, own, steps=1):
        p = q * halves + k
        return pltpu.make_async_remote_copy(
            src_ref=source(shard, q, k, own),
            dst_ref=piece(shard, q, k),
            send_sem=o_send.at[way, steps - 1, p] if own else z_send.at[way, shard, p],
            recv_sem=z_recv.at[shard, p],
            device_id=(s, t + steps if way == 0 else t - steps),
            device_id_type=MESH,
        )

    def c_copy(shard, q, k, own):
        return pltpu.make_async_remote_copy(
            src_ref=source(shard, q, k, own),
            dst_ref=cols.at[pl.ds(pl.multiple_of(s * tokens + q * part, part), part), :],
            send_sem=c_send.at[shard, q * halves + k],
            recv_sem=c_recv.at[s, q],
            device_id=(shard * halves + k, t),
            device_id_type=MESH,
        )

    def z_go(shard, q, k, way, own, steps=1):
        @pl.when(t + steps < n_tensor if way == 0 else t >= steps)
        def _():
            z_copy(shard, q, k, way, own, steps).start()

    def c_go(shard, q, k, own):
        @pl.when(shard * halves + k != s)
        def _():
            c_copy(shard, q, k, own).start()

    def w_copy(i):
        return pltpu.make_async_remote_copy(
            src_ref=scaled.at[pl.ds(pl.multiple_of(s * tokens, tokens), tokens), :],
            dst_ref=scaled.at[pl.ds(pl.multiple_of(s * tokens, tokens), tokens), :],
            send_sem=w_send.at[i],
            recv_sem=w_recv.at[s],
            device_id=(sibling if i == 0 else lax.rem(s + 2 * i, n_seq), t),
            device_id_type=MESH,
        )

    def f_copy(i):
        origin = lax.rem(s + n_seq - 2 * i, n_seq)
        at = scaled.at[pl.ds(pl.multiple_of(origin * tokens, tokens), tokens), :]
        return pltpu.make_async_remote_copy(
            src_ref=at, dst_ref=at, send_sem=f_send.at[i], recv_sem=w_recv.at[origin],
            device_id=(sibling, t), device_id_type=MESH,
        )

    def multiply(shard, q, k):
        left = rows[shard, k, q * part : (q + 1) * part, :]
        at = pl.ds(pl.multiple_of((shard * halves + k) * block, block), block)
        for e in range(experts):
            raw[q * part : (q + 1) * part, e * hidden : (e + 1) * hidden] += lax.dot_general(
                left, weight[e, :, at], (((1,), (1,)), ((), ())), preferred_element_type=jnp.float32
            )

    def send_own(p):
        q, k = rounds[p]
        for steps in range(reach, 0, -1):
            z_go(t, q, k, 0, True, steps)
            z_go(t, q, k, 1, True, steps)
        c_go(t, q, k, True)

    for p in range(min(AHEAD + 1, len(rounds))):
        send_own(p)

    for copy in first_copies:
        copy.wait()
    for e in range(experts):
        hot, live = token_slots(tok_ref, count_ref, e, tokens)
        ordered = jnp.dot(hot.astype(jnp.bfloat16), pre[e], preferred_element_type=jnp.float32)
        probs = jnp.sum(jnp.where(live, prob_ref[e : e + 1, :], 0.0), axis=1, keepdims=True)
        gate, up = ordered[:, :hidden], ordered[:, hidden:]
        sigma = jax.nn.sigmoid(gate)
        silu = gate * sigma
        active = (silu * up).astype(jnp.bfloat16)
        act[:, e * hidden : (e + 1) * hidden] = active
        scaled[pl.ds(pl.multiple_of(s * tokens, tokens), tokens), e * hidden : (e + 1) * hidden] = (
            probs * active.astype(jnp.float32)
        ).astype(jnp.bfloat16)
        coef[e, :, :hidden] = probs * up * sigma * (1.0 + gate * (1.0 - sigma))
        coef[e, :, hidden:] = probs * silu
    for i in range(1, n_seq // 2):
        w_copy(i).start()
    w_copy(0).start()
    raw[...] = jnp.zeros_like(raw)
    for copy in own_copies:
        copy.wait()
    weight_copy.wait()

    def add_groups(q, first):
        for g in range(n_seq):
            at = pl.ds(g * tokens + q * part, part)
            term = lax.dot_general(
                scaled[at, :], cols[at, :], (((0,), (0,)), ((), ())), preferred_element_type=jnp.float32
            )
            if first and g == 0:
                total[...] = term
            else:
                total[...] += term

    def wait_groups(q):
        for g in range(n_seq):
            @pl.when(g != s)
            def _():
                at = cols.at[pl.ds(g * tokens + q * part, part), :]
                pltpu.make_async_remote_copy(
                    src_ref=at, dst_ref=at, send_sem=c_send.at[0, 0], recv_sem=c_recv.at[g, q],
                    device_id=(sibling, t), device_id_type=MESH,
                ).wait_recv()

    def use(shard, q, k):
        c_go(shard, q, k, False)
        multiply(shard, q, k)

    for tick in range(len(rounds) + n_tensor - 1 - reach):
        if tick > 0 and tick + AHEAD < len(rounds):
            send_own(tick + AHEAD)
        for d in range(1, n_tensor):
            p = tick - max(0, d - reach)
            if not 0 <= p < len(rounds):
                continue
            q, k = rounds[p]

            @pl.when(t >= d)
            def _():
                z_copy(t - d, q, k, 1, False).wait_recv()
                if d >= reach:
                    z_go(t - d, q, k, 0, False)
                use(t - d, q, k)

            @pl.when(t + d < n_tensor)
            def _():
                z_copy(t + d, q, k, 0, False).wait_recv()
                if d >= reach:
                    z_go(t + d, q, k, 1, False)
                use(t + d, q, k)

        if tick < len(rounds):
            multiply(t, *rounds[tick])
        if tick == min(1, len(rounds) - 1):
            for i in range(1, n_seq // 2):
                f_copy(i).wait_recv()
                f_copy(i).start()

    cols[pl.ds(pl.multiple_of(s * tokens, tokens), tokens), :] = rows[lax.div(s, halves), lax.rem(s, halves)]
    for e in range(experts):
        hot, live = token_slots(tok_ref, count_ref, e, tokens)
        part_raw = raw[:, e * hidden : (e + 1) * hidden]
        grads = jnp.concatenate(
            [coef[e, :, :hidden] * part_raw, coef[e, :, hidden:] * part_raw], axis=1
        ).astype(jnp.bfloat16)
        pre_out[0, e] = lax.dot_general(
            hot.astype(jnp.bfloat16), grads, (((0,), (0,)), ((), ())), preferred_element_type=jnp.float32
        ).astype(jnp.bfloat16)
        sums = jnp.sum(
            act[:, e * hidden : (e + 1) * hidden].astype(jnp.float32) * part_raw, axis=1, keepdims=True
        )
        prob_out[0, e : e + 1, :] = jnp.sum(jnp.where(live, sums, 0.0), axis=0, keepdims=True)

    for g in range(n_seq):
        @pl.when(lax.rem(g, 2) != lax.rem(s, 2))
        def _():
            at = scaled.at[pl.ds(g * tokens, tokens), :]
            pltpu.make_async_remote_copy(
                src_ref=at, dst_ref=at, send_sem=w_send.at[0], recv_sem=w_recv.at[g],
                device_id=(sibling, t), device_id_type=MESH,
            ).wait_recv()
    for q in range(PIECES):
        wait_groups(q)
        add_groups(q, q == 0)
    for e in range(experts):
        weight_out[e] = total[e * hidden : (e + 1) * hidden, :].astype(jnp.bfloat16)

    for i in range(n_seq // 2):
        w_copy(i).wait_send()
    for i in range(1, n_seq // 2):
        f_copy(i).wait_send()
    for shard in range(n_tensor):
        for q, k in rounds:
            @pl.when(shard * halves + k != s)
            def _():
                c_copy(shard, q, k, False).wait_send()

            @pl.when((shard + reach <= t) & (t < n_tensor - 1))
            def _():
                z_copy(shard, q, k, 0, False).wait_send()

            @pl.when((shard - reach >= t) & (t > 0))
            def _():
                z_copy(shard, q, k, 1, False).wait_send()

    for q, k in rounds:
        for steps in range(1, reach + 1):
            @pl.when(t + steps < n_tensor)
            def _():
                z_copy(t, q, k, 0, True, steps).wait_send()

            @pl.when(t >= steps)
            def _():
                z_copy(t, q, k, 1, True, steps).wait_send()


def per_device(n_seq, n_tensor, out_grad, down_weight, pre_act, gate_prob, slot_token, slot_count):
    tokens, shard = out_grad.shape
    experts, hidden, width = down_weight.shape
    block = width // n_seq
    halves = n_seq // n_tensor
    pieces = PIECES * halves
    reach = min(DIRECT, n_tensor - 1)
    whole = pl.BlockSpec(memory_space=pltpu.VMEM)
    away = pl.BlockSpec(memory_space=pltpu.HBM)
    dma = pltpu.SemaphoreType.DMA
    return pl.pallas_call(
        functools.partial(kernel, n_seq, n_tensor),
        out_shape=(
            jax.ShapeDtypeStruct((1, experts, tokens, 2 * hidden), jnp.bfloat16),
            jax.ShapeDtypeStruct((1, experts, tokens), jnp.float32),
            jax.ShapeDtypeStruct((experts, hidden, block), jnp.bfloat16),
        ),
        in_specs=[away] * 6,
        out_specs=(whole, whole, whole),
        scratch_shapes=[
            pltpu.SMEM((1, experts), jnp.int32),
            pltpu.VMEM((experts, tokens), jnp.int32),
            pltpu.VMEM((experts, tokens), jnp.float32),
            pltpu.VMEM((n_tensor, halves, tokens, block), jnp.bfloat16),
            pltpu.VMEM((n_seq * tokens, block), jnp.bfloat16),
            pltpu.VMEM((n_seq * tokens, experts * hidden), jnp.bfloat16),
            pltpu.VMEM((experts, hidden, width), jnp.bfloat16),
            pltpu.VMEM((experts, tokens, 2 * hidden), jnp.bfloat16),
            pltpu.VMEM((experts, tokens, 2 * hidden), jnp.float32),
            pltpu.VMEM((tokens, experts * hidden), jnp.bfloat16),
            pltpu.VMEM((tokens, experts * hidden), jnp.float32),
            pltpu.VMEM((experts * hidden, block), jnp.float32),
            dma((5 + halves,)),
            dma((2, reach, pieces)),
            dma((2, n_tensor, pieces)),
            dma((n_tensor, pieces)),
            dma((n_tensor, pieces)),
            dma((n_seq, PIECES)),
            dma((n_seq // 2,)),
            dma((n_seq,)),
            dma((n_seq // 2,)),
        ],
        compiler_params=pltpu.CompilerParams(
            collective_id=0, has_side_effects=True, vmem_limit_bytes=40 * 1024 * 1024
        ),
    )(
        *[
            pltpu.with_memory_space_constraint(operand, pltpu.HBM)
            for operand in (slot_count, slot_token, gate_prob, out_grad, down_weight, pre_act)
        ]
    )


def solution(mesh):
    placed = (
        P("seq", "tensor"),
        P("tensor", None, None),
        P("seq", "tensor", None, None),
        P("seq", "tensor", None),
        P("seq", "tensor", None),
        P("seq", "tensor"),
    )
    return jax.shard_map(
        functools.partial(per_device, mesh.shape["seq"], mesh.shape["tensor"]),
        mesh=mesh,
        in_specs=placed,
        out_specs=(
            P("seq", "tensor", None, None),
            P("seq", "tensor", None),
            P("tensor", None, "seq"),
        ),
        check_vma=False,
    )
```

```python
import functools

import jax
import jax.numpy as jnp
from jax import lax
from jax.experimental import pallas as pl
from jax.experimental.pallas import tpu as pltpu
from jax.sharding import PartitionSpec as P

MESH = pl.DeviceIdType.MESH
PIECES = 2
AHEAD = 1
EARLY = 2
DIRECT = 1


def token_slots(tok_ref, count_ref, expert, tokens):
    token = lax.broadcasted_iota(jnp.int32, (tokens, tokens), 0)
    slot = lax.broadcasted_iota(jnp.int32, (tokens, tokens), 1)
    hot = token == tok_ref[expert : expert + 1, :]
    return hot, hot & (slot < count_ref[0, expert])


def kernel(
    n_seq, n_tensor,
    count_in, tok_in, prob_in, grad_ref, weight_ref, pre_ref,
    pre_out, prob_out, weight_out,
    count_ref, tok_ref, prob_ref, rows, cols, scaled, weight, pre, coef, act, raw, total,
    local_sem, o_send, z_send, z_recv, c_send, c_recv, w_send, w_recv, f_send,
):
    s = lax.axis_index("seq")
    t = lax.axis_index("tensor")
    experts, hidden, _ = weight_ref.shape
    tokens = grad_ref.shape[0]
    block = cols.shape[2]
    halves = n_seq // n_tensor
    part = tokens // PIECES
    reach = min(DIRECT, n_tensor - 1)
    rounds = [(q, k) for q in range(PIECES) for k in range(halves)]
    sibling = s + 1 - 2 * lax.rem(s, 2)

    barrier = pltpu.get_barrier_semaphore()
    for i in range(1, n_seq):
        pl.semaphore_signal(barrier, inc=1, device_id=(lax.rem(s + i, n_seq), t), device_id_type=MESH)

    greeted = n_seq - 1
    for steps in range(1, reach + 1):
        @pl.when(t >= steps)
        def _():
            pl.semaphore_signal(barrier, inc=1, device_id=(s, t - steps), device_id_type=MESH)

        @pl.when(t + steps < n_tensor)
        def _():
            pl.semaphore_signal(barrier, inc=1, device_id=(s, t + steps), device_id_type=MESH)

        greeted += (t >= steps).astype(jnp.int32) + (t + steps < n_tensor).astype(jnp.int32)

    first_copies = [
        pltpu.make_async_copy(pre_ref.at[0], pre, local_sem.at[0]),
        pltpu.make_async_copy(count_in, count_ref, local_sem.at[1]),
        pltpu.make_async_copy(tok_in.at[0], tok_ref, local_sem.at[2]),
        pltpu.make_async_copy(prob_in.at[0], prob_ref, local_sem.at[3]),
    ]
    for copy in first_copies:
        copy.start()
    own_copies = []
    for k in range(halves):
        own_copies.append(
            pltpu.make_async_copy(
                grad_ref.at[:, pl.ds(k * block, block)], rows.at[t, k], local_sem.at[5 + k]
            )
        )
        own_copies[-1].start()
    weight_copy = pltpu.make_async_copy(weight_ref, weight, local_sem.at[4])
    weight_copy.start()
    pl.semaphore_wait(barrier, greeted)

    def piece(shard, q, k):
        return rows.at[shard, k, pl.ds(q * part, part), :]

    def source(shard, q, k, own):
        if own:
            return grad_ref.at[pl.ds(q * part, part), pl.ds(k * block, block)]
        return piece(shard, q, k)

    def z_copy(shard, q, k, way, own, steps=1):
        p = q * halves + k
        return pltpu.make_async_remote_copy(
            src_ref=source(shard, q, k, own),
            dst_ref=piece(shard, q, k),
            send_sem=o_send.at[way, steps - 1, p] if own else z_send.at[way, shard, p],
            recv_sem=z_recv.at[shard, p],
            device_id=(s, t + steps if way == 0 else t - steps),
            device_id_type=MESH,
        )

    def c_copy(shard, q, k, own):
        return pltpu.make_async_remote_copy(
            src_ref=source(shard, q, k, own),
            dst_ref=cols.at[q, pl.ds(pl.multiple_of(s * part, part), part), :],
            send_sem=c_send.at[shard, q * halves + k],
            recv_sem=c_recv.at[s, q],
            device_id=(shard * halves + k, t),
            device_id_type=MESH,
        )

    def z_go(shard, q, k, way, own, steps=1):
        @pl.when(t + steps < n_tensor if way == 0 else t >= steps)
        def _():
            z_copy(shard, q, k, way, own, steps).start()

    def c_go(shard, q, k, own):
        @pl.when(shard * halves + k != s)
        def _():
            c_copy(shard, q, k, own).start()

    def group(origin):
        return scaled.at[:, pl.ds(pl.multiple_of(origin * part, part), part), :]

    def w_copy(i):
        return pltpu.make_async_remote_copy(
            src_ref=group(s),
            dst_ref=group(s),
            send_sem=w_send.at[i],
            recv_sem=w_recv.at[s],
            device_id=(sibling if i == 0 else lax.rem(s + 2 * i, n_seq), t),
            device_id_type=MESH,
        )

    def f_copy(i):
        origin = lax.rem(s + n_seq - 2 * i, n_seq)
        at = group(origin)
        return pltpu.make_async_remote_copy(
            src_ref=at, dst_ref=at, send_sem=f_send.at[i], recv_sem=w_recv.at[origin],
            device_id=(sibling, t), device_id_type=MESH,
        )

    def multiply(shard, q, k):
        left = rows[shard, k, q * part : (q + 1) * part, :]
        at = pl.ds(pl.multiple_of((shard * halves + k) * block, block), block)
        for e in range(experts):
            raw[q * part : (q + 1) * part, e * hidden : (e + 1) * hidden] += lax.dot_general(
                left, weight[e, :, at], (((1,), (1,)), ((), ())), preferred_element_type=jnp.float32
            )

    def send_own(p):
        q, k = rounds[p]
        for steps in range(reach, 0, -1):
            z_go(t, q, k, 0, True, steps)
            z_go(t, q, k, 1, True, steps)
        c_go(t, q, k, True)

    for p in range(min(AHEAD + 1, len(rounds))):
        send_own(p)

    def prepare(e):
        hot, live = token_slots(tok_ref, count_ref, e, tokens)
        ordered = jnp.dot(hot.astype(jnp.bfloat16), pre[e], preferred_element_type=jnp.float32)
        probs = jnp.sum(jnp.where(live, prob_ref[e : e + 1, :], 0.0), axis=1, keepdims=True)
        gate, up = ordered[:, :hidden], ordered[:, hidden:]
        sigma = jax.nn.sigmoid(gate)
        silu = gate * sigma
        active = (silu * up).astype(jnp.bfloat16)
        act[:, e * hidden : (e + 1) * hidden] = active
        weighted = (probs * active.astype(jnp.float32)).astype(jnp.bfloat16)
        for q in range(PIECES):
            scaled[
                q, pl.ds(pl.multiple_of(s * part, part), part), e * hidden : (e + 1) * hidden
            ] = weighted[q * part : (q + 1) * part]
        coef[e, :, :hidden] = probs * up * sigma * (1.0 + gate * (1.0 - sigma))
        coef[e, :, hidden:] = probs * silu

    def add_groups(q):
        for e in range(experts):
            term = lax.dot_general(
                scaled[q, :, e * hidden : (e + 1) * hidden], cols[q],
                (((0,), (0,)), ((), ())), preferred_element_type=jnp.float32,
            )
            if q > 0:
                term += total[e]
            if q < PIECES - 1:
                total[e] = term
            else:
                weight_out[e] = term.astype(jnp.bfloat16)

    def wait_weighted():
        for g in range(n_seq):
            @pl.when(lax.rem(g, 2) != lax.rem(s, 2))
            def _():
                at = group(g)
                pltpu.make_async_remote_copy(
                    src_ref=at, dst_ref=at, send_sem=w_send.at[0], recv_sem=w_recv.at[g],
                    device_id=(sibling, t), device_id_type=MESH,
                ).wait_recv()

    def wait_groups(q):
        for g in range(n_seq):
            @pl.when(g != s)
            def _():
                at = cols.at[q, pl.ds(g * part, part), :]
                pltpu.make_async_remote_copy(
                    src_ref=at, dst_ref=at, send_sem=c_send.at[0, 0], recv_sem=c_recv.at[g, q],
                    device_id=(sibling, t), device_id_type=MESH,
                ).wait_recv()

    def own_block(q):
        at = pl.ds(pl.multiple_of(s * part, part), part)
        cols[q, at, :] = rows[lax.div(s, halves), lax.rem(s, halves), q * part : (q + 1) * part, :]

    ticks = len(rounds) + n_tensor - 1 - reach
    for tick in range(ticks):
        if tick > 0 and tick + AHEAD < len(rounds):
            send_own(tick + AHEAD)
        taken = []
        for d in range(n_tensor - 1, 0, -1):
            p = tick - max(0, d - reach)
            if 0 <= p < len(rounds):
                taken.append((d, *rounds[p]))
        for d, q, k in taken:
            @pl.when(t >= d)
            def _():
                z_copy(t - d, q, k, 1, False).wait_recv()
                if d >= reach:
                    z_go(t - d, q, k, 0, False)
                c_go(t - d, q, k, False)

            @pl.when(t + d < n_tensor)
            def _():
                z_copy(t + d, q, k, 0, False).wait_recv()
                if d >= reach:
                    z_go(t + d, q, k, 1, False)
                c_go(t + d, q, k, False)

        if tick == 0:
            for copy in first_copies:
                copy.wait()
        for e in range(experts):
            if tick == 0:
                prepare(e)
        if tick == 0:
            for i in range(1, n_seq // 2):
                w_copy(i).start()
            w_copy(0).start()
        if tick == 0:
            for copy in own_copies:
                copy.wait()
            weight_copy.wait()
            raw[...] = jnp.zeros_like(raw)
        for d, q, k in taken:
            @pl.when(t >= d)
            def _():
                multiply(t - d, q, k)

            @pl.when(t + d < n_tensor)
            def _():
                multiply(t + d, q, k)

        if tick < len(rounds):
            multiply(t, *rounds[tick])
        if tick == min(2, ticks - 1):
            for i in range(1, n_seq // 2):
                f_copy(i).wait_recv()
                f_copy(i).start()
        if tick == ticks - EARLY:
            wait_weighted()
            for q in range(PIECES - 1):
                wait_groups(q)
                own_block(q)
                add_groups(q)

    own_block(PIECES - 1)
    for e in range(experts):
        hot, live = token_slots(tok_ref, count_ref, e, tokens)
        part_raw = raw[:, e * hidden : (e + 1) * hidden]
        grads = jnp.concatenate(
            [coef[e, :, :hidden] * part_raw, coef[e, :, hidden:] * part_raw], axis=1
        ).astype(jnp.bfloat16)
        pre_out[0, e] = lax.dot_general(
            hot.astype(jnp.bfloat16), grads, (((0,), (0,)), ((), ())), preferred_element_type=jnp.float32
        ).astype(jnp.bfloat16)
        sums = jnp.sum(
            act[:, e * hidden : (e + 1) * hidden].astype(jnp.float32) * part_raw, axis=1, keepdims=True
        )
        prob_out[0, e : e + 1, :] = jnp.sum(jnp.where(live, sums, 0.0), axis=0, keepdims=True)

    wait_groups(PIECES - 1)
    add_groups(PIECES - 1)

    for i in range(n_seq // 2):
        w_copy(i).wait_send()
    for i in range(1, n_seq // 2):
        f_copy(i).wait_send()
    for shard in range(n_tensor):
        for q, k in rounds:
            @pl.when(shard * halves + k != s)
            def _():
                c_copy(shard, q, k, False).wait_send()

            @pl.when((shard + reach <= t) & (t < n_tensor - 1))
            def _():
                z_copy(shard, q, k, 0, False).wait_send()

            @pl.when((shard - reach >= t) & (t > 0))
            def _():
                z_copy(shard, q, k, 1, False).wait_send()

    for q, k in rounds:
        for steps in range(1, reach + 1):
            @pl.when(t + steps < n_tensor)
            def _():
                z_copy(t, q, k, 0, True, steps).wait_send()

            @pl.when(t >= steps)
            def _():
                z_copy(t, q, k, 1, True, steps).wait_send()


def per_device(n_seq, n_tensor, out_grad, down_weight, pre_act, gate_prob, slot_token, slot_count):
    tokens, shard = out_grad.shape
    experts, hidden, width = down_weight.shape
    block = width // n_seq
    halves = n_seq // n_tensor
    pieces = PIECES * halves
    reach = min(DIRECT, n_tensor - 1)
    whole = pl.BlockSpec(memory_space=pltpu.VMEM)
    away = pl.BlockSpec(memory_space=pltpu.HBM)
    dma = pltpu.SemaphoreType.DMA
    return pl.pallas_call(
        functools.partial(kernel, n_seq, n_tensor),
        out_shape=(
            jax.ShapeDtypeStruct((1, experts, tokens, 2 * hidden), jnp.bfloat16),
            jax.ShapeDtypeStruct((1, experts, tokens), jnp.float32),
            jax.ShapeDtypeStruct((experts, hidden, block), jnp.bfloat16),
        ),
        in_specs=[away] * 6,
        out_specs=(whole, whole, whole),
        scratch_shapes=[
            pltpu.SMEM((1, experts), jnp.int32),
            pltpu.VMEM((experts, tokens), jnp.int32),
            pltpu.VMEM((experts, tokens), jnp.float32),
            pltpu.VMEM((n_tensor, halves, tokens, block), jnp.bfloat16),
            pltpu.VMEM((PIECES, n_seq * tokens // PIECES, block), jnp.bfloat16),
            pltpu.VMEM((PIECES, n_seq * tokens // PIECES, experts * hidden), jnp.bfloat16),
            pltpu.VMEM((experts, hidden, width), jnp.bfloat16),
            pltpu.VMEM((experts, tokens, 2 * hidden), jnp.bfloat16),
            pltpu.VMEM((experts, tokens, 2 * hidden), jnp.float32),
            pltpu.VMEM((tokens, experts * hidden), jnp.bfloat16),
            pltpu.VMEM((tokens, experts * hidden), jnp.float32),
            pltpu.VMEM((experts, hidden, block), jnp.float32),
            dma((5 + halves,)),
            dma((2, reach, pieces)),
            dma((2, n_tensor, pieces)),
            dma((n_tensor, pieces)),
            dma((n_tensor, pieces)),
            dma((n_seq, PIECES)),
            dma((n_seq // 2,)),
            dma((n_seq,)),
            dma((n_seq // 2,)),
        ],
        compiler_params=pltpu.CompilerParams(
            collective_id=0, has_side_effects=True, vmem_limit_bytes=40 * 1024 * 1024
        ),
    )(
        *[
            pltpu.with_memory_space_constraint(operand, pltpu.HBM)
            for operand in (slot_count, slot_token, gate_prob, out_grad, down_weight, pre_act)
        ]
    )


def solution(mesh):
    placed = (
        P("seq", "tensor"),
        P("tensor", None, None),
        P("seq", "tensor", None, None),
        P("seq", "tensor", None),
        P("seq", "tensor", None),
        P("seq", "tensor"),
    )
    return jax.shard_map(
        functools.partial(per_device, mesh.shape["seq"], mesh.shape["tensor"]),
        mesh=mesh,
        in_specs=placed,
        out_specs=(
            P("seq", "tensor", None, None),
            P("seq", "tensor", None),
            P("tensor", None, "seq"),
        ),
        check_vma=False,
    )
```

```python
import functools

import jax
import jax.numpy as jnp
from jax import lax
from jax.experimental import pallas as pl
from jax.experimental.pallas import tpu as pltpu
from jax.sharding import PartitionSpec as P

MESH = pl.DeviceIdType.MESH
PIECES = 2
AHEAD = 1
EARLY = 2
DIRECT = 1


def token_slots(tok_ref, count_ref, expert, tokens):
    token = lax.broadcasted_iota(jnp.int32, (tokens, tokens), 0)
    slot = lax.broadcasted_iota(jnp.int32, (tokens, tokens), 1)
    hot = token == tok_ref[expert : expert + 1, :]
    return hot, hot & (slot < count_ref[0, expert])


def kernel(
    n_seq, n_tensor,
    count_in, tok_in, prob_in, grad_ref, weight_ref, pre_ref,
    pre_out, prob_out, weight_out,
    count_ref, tok_ref, prob_ref, rows, cols, scaled, weight, pre, coef, act, raw, total,
    local_sem, o_send, z_send, z_recv, c_send, c_recv, w_send, w_recv, f_send,
):
    s = lax.axis_index("seq")
    t = lax.axis_index("tensor")
    experts, hidden, _ = weight_ref.shape
    tokens = grad_ref.shape[0]
    block = cols.shape[2]
    halves = n_seq // n_tensor
    part = tokens // PIECES
    reach = min(DIRECT, n_tensor - 1)
    rounds = [(q, k) for q in range(PIECES) for k in range(halves)]
    sibling = s + 1 - 2 * lax.rem(s, 2)

    barrier = pltpu.get_barrier_semaphore()
    for i in range(1, n_seq):
        pl.semaphore_signal(barrier, inc=1, device_id=(lax.rem(s + i, n_seq), t), device_id_type=MESH)

    greeted = n_seq - 1
    for steps in range(1, reach + 1):
        @pl.when(t >= steps)
        def _():
            pl.semaphore_signal(barrier, inc=1, device_id=(s, t - steps), device_id_type=MESH)

        @pl.when(t + steps < n_tensor)
        def _():
            pl.semaphore_signal(barrier, inc=1, device_id=(s, t + steps), device_id_type=MESH)

        greeted += (t >= steps).astype(jnp.int32) + (t + steps < n_tensor).astype(jnp.int32)

    first_copies = [
        pltpu.make_async_copy(pre_ref.at[0], pre, local_sem.at[0]),
        pltpu.make_async_copy(count_in, count_ref, local_sem.at[1]),
        pltpu.make_async_copy(tok_in.at[0], tok_ref, local_sem.at[2]),
        pltpu.make_async_copy(prob_in.at[0], prob_ref, local_sem.at[3]),
    ]
    for copy in first_copies:
        copy.start()
    own_copies = []
    for k in range(halves):
        own_copies.append(
            pltpu.make_async_copy(
                grad_ref.at[:, pl.ds(k * block, block)], rows.at[t, k], local_sem.at[5 + k]
            )
        )
        own_copies[-1].start()
    weight_copy = pltpu.make_async_copy(weight_ref, weight, local_sem.at[4])
    weight_copy.start()
    pl.semaphore_wait(barrier, greeted)

    def piece(shard, q, k):
        return rows.at[shard, k, pl.ds(q * part, part), :]

    def source(shard, q, k, own):
        if own:
            return grad_ref.at[pl.ds(q * part, part), pl.ds(k * block, block)]
        return piece(shard, q, k)

    def z_copy(shard, q, k, way, own, steps=1):
        p = q * halves + k
        return pltpu.make_async_remote_copy(
            src_ref=source(shard, q, k, own),
            dst_ref=piece(shard, q, k),
            send_sem=o_send.at[way, steps - 1, p] if own else z_send.at[way, shard, p],
            recv_sem=z_recv.at[shard, p],
            device_id=(s, t + steps if way == 0 else t - steps),
            device_id_type=MESH,
        )

    def c_copy(shard, q, k, own):
        return pltpu.make_async_remote_copy(
            src_ref=source(shard, q, k, own),
            dst_ref=cols.at[q, pl.ds(pl.multiple_of(s * part, part), part), :],
            send_sem=c_send.at[shard, q * halves + k],
            recv_sem=c_recv.at[s, q],
            device_id=(shard * halves + k, t),
            device_id_type=MESH,
        )

    def z_go(shard, q, k, way, own, steps=1):
        @pl.when(t + steps < n_tensor if way == 0 else t >= steps)
        def _():
            z_copy(shard, q, k, way, own, steps).start()

    def c_go(shard, q, k, own):
        @pl.when(shard * halves + k != s)
        def _():
            c_copy(shard, q, k, own).start()

    def group(origin):
        return scaled.at[:, pl.ds(pl.multiple_of(origin * part, part), part), :]

    def w_copy(i):
        return pltpu.make_async_remote_copy(
            src_ref=group(s),
            dst_ref=group(s),
            send_sem=w_send.at[i],
            recv_sem=w_recv.at[s],
            device_id=(sibling if i == 0 else lax.rem(s + 2 * i, n_seq), t),
            device_id_type=MESH,
        )

    def f_copy(i):
        origin = lax.rem(s + n_seq - 2 * i, n_seq)
        at = group(origin)
        return pltpu.make_async_remote_copy(
            src_ref=at, dst_ref=at, send_sem=f_send.at[i], recv_sem=w_recv.at[origin],
            device_id=(sibling, t), device_id_type=MESH,
        )

    def multiply(shard, q, k):
        left = rows[shard, k, q * part : (q + 1) * part, :]
        at = pl.ds(pl.multiple_of((shard * halves + k) * block, block), block)
        for e in range(experts):
            raw[q * part : (q + 1) * part, e * hidden : (e + 1) * hidden] += lax.dot_general(
                left, weight[e, :, at], (((1,), (1,)), ((), ())), preferred_element_type=jnp.float32
            )

    def send_own(p):
        q, k = rounds[p]
        for steps in range(reach, 0, -1):
            z_go(t, q, k, 0, True, steps)
            z_go(t, q, k, 1, True, steps)
        c_go(t, q, k, True)

    for p in range(min(AHEAD + 1, len(rounds))):
        send_own(p)

    def prepare(e):
        hot, live = token_slots(tok_ref, count_ref, e, tokens)
        ordered = jnp.dot(hot.astype(jnp.bfloat16), pre[e], preferred_element_type=jnp.float32)
        probs = jnp.sum(jnp.where(live, prob_ref[e : e + 1, :], 0.0), axis=1, keepdims=True)
        gate, up = ordered[:, :hidden], ordered[:, hidden:]
        sigma = jax.nn.sigmoid(gate)
        silu = gate * sigma
        active = (silu * up).astype(jnp.bfloat16)
        act[:, e * hidden : (e + 1) * hidden] = active
        weighted = (probs * active.astype(jnp.float32)).astype(jnp.bfloat16)
        for q in range(PIECES):
            scaled[
                q, pl.ds(pl.multiple_of(s * part, part), part), e * hidden : (e + 1) * hidden
            ] = weighted[q * part : (q + 1) * part]
        coef[e, :, :hidden] = probs * up * sigma * (1.0 + gate * (1.0 - sigma))
        coef[e, :, hidden:] = probs * silu

    def add_groups(q):
        for e in range(experts):
            term = lax.dot_general(
                scaled[q, :, e * hidden : (e + 1) * hidden], cols[q],
                (((0,), (0,)), ((), ())), preferred_element_type=jnp.float32,
            )
            if q > 0:
                term += total[e]
            if q < PIECES - 1:
                total[e] = term
            else:
                weight_out[e] = term.astype(jnp.bfloat16)

    def wait_weighted():
        for g in range(n_seq):
            @pl.when(lax.rem(g, 2) != lax.rem(s, 2))
            def _():
                at = group(g)
                pltpu.make_async_remote_copy(
                    src_ref=at, dst_ref=at, send_sem=w_send.at[0], recv_sem=w_recv.at[g],
                    device_id=(sibling, t), device_id_type=MESH,
                ).wait_recv()

    def wait_groups(q):
        for g in range(n_seq):
            @pl.when(g != s)
            def _():
                at = cols.at[q, pl.ds(g * part, part), :]
                pltpu.make_async_remote_copy(
                    src_ref=at, dst_ref=at, send_sem=c_send.at[0, 0], recv_sem=c_recv.at[g, q],
                    device_id=(sibling, t), device_id_type=MESH,
                ).wait_recv()

    def own_block(q):
        at = pl.ds(pl.multiple_of(s * part, part), part)
        cols[q, at, :] = rows[lax.div(s, halves), lax.rem(s, halves), q * part : (q + 1) * part, :]

    ticks = len(rounds) + n_tensor - 1 - reach
    for tick in range(ticks):
        if tick > 0 and tick + AHEAD < len(rounds):
            send_own(tick + AHEAD)
        if tick == 0:
            for copy in first_copies:
                copy.wait()
        for e in range(experts):
            if tick == 0:
                prepare(e)
        if tick == 0:
            for i in range(1, n_seq // 2):
                w_copy(i).start()
            w_copy(0).start()
        taken = []
        for d in range(n_tensor - 1, 0, -1):
            p = tick - max(0, d - reach)
            if 0 <= p < len(rounds):
                taken.append((d, *rounds[p]))
        for d, q, k in taken:
            @pl.when(t >= d)
            def _():
                z_copy(t - d, q, k, 1, False).wait_recv()
                if d >= reach:
                    z_go(t - d, q, k, 0, False)
                c_go(t - d, q, k, False)

            @pl.when(t + d < n_tensor)
            def _():
                z_copy(t + d, q, k, 0, False).wait_recv()
                if d >= reach:
                    z_go(t + d, q, k, 1, False)
                c_go(t + d, q, k, False)

        if tick == 0:
            for copy in own_copies:
                copy.wait()
            weight_copy.wait()
            raw[...] = jnp.zeros_like(raw)
        for d, q, k in taken:
            @pl.when(t >= d)
            def _():
                multiply(t - d, q, k)

            @pl.when(t + d < n_tensor)
            def _():
                multiply(t + d, q, k)

        if tick < len(rounds):
            multiply(t, *rounds[tick])
        if tick == min(2, ticks - 1):
            for i in range(1, n_seq // 2):
                f_copy(i).wait_recv()
                f_copy(i).start()
        if tick == ticks - EARLY:
            wait_weighted()
            for q in range(PIECES - 1):
                wait_groups(q)
                own_block(q)
                add_groups(q)

    own_block(PIECES - 1)
    for e in range(experts):
        hot, live = token_slots(tok_ref, count_ref, e, tokens)
        part_raw = raw[:, e * hidden : (e + 1) * hidden]
        grads = jnp.concatenate(
            [coef[e, :, :hidden] * part_raw, coef[e, :, hidden:] * part_raw], axis=1
        ).astype(jnp.bfloat16)
        pre_out[0, e] = lax.dot_general(
            hot.astype(jnp.bfloat16), grads, (((0,), (0,)), ((), ())), preferred_element_type=jnp.float32
        ).astype(jnp.bfloat16)
        sums = jnp.sum(
            act[:, e * hidden : (e + 1) * hidden].astype(jnp.float32) * part_raw, axis=1, keepdims=True
        )
        prob_out[0, e : e + 1, :] = jnp.sum(jnp.where(live, sums, 0.0), axis=0, keepdims=True)

    wait_groups(PIECES - 1)
    add_groups(PIECES - 1)

    for i in range(n_seq // 2):
        w_copy(i).wait_send()
    for i in range(1, n_seq // 2):
        f_copy(i).wait_send()
    for shard in range(n_tensor):
        for q, k in rounds:
            @pl.when(shard * halves + k != s)
            def _():
                c_copy(shard, q, k, False).wait_send()

            @pl.when((shard + reach <= t) & (t < n_tensor - 1))
            def _():
                z_copy(shard, q, k, 0, False).wait_send()

            @pl.when((shard - reach >= t) & (t > 0))
            def _():
                z_copy(shard, q, k, 1, False).wait_send()

    for q, k in rounds:
        for steps in range(1, reach + 1):
            @pl.when(t + steps < n_tensor)
            def _():
                z_copy(t, q, k, 0, True, steps).wait_send()

            @pl.when(t >= steps)
            def _():
                z_copy(t, q, k, 1, True, steps).wait_send()


def per_device(n_seq, n_tensor, out_grad, down_weight, pre_act, gate_prob, slot_token, slot_count):
    tokens, shard = out_grad.shape
    experts, hidden, width = down_weight.shape
    block = width // n_seq
    halves = n_seq // n_tensor
    pieces = PIECES * halves
    reach = min(DIRECT, n_tensor - 1)
    whole = pl.BlockSpec(memory_space=pltpu.VMEM)
    away = pl.BlockSpec(memory_space=pltpu.HBM)
    dma = pltpu.SemaphoreType.DMA
    return pl.pallas_call(
        functools.partial(kernel, n_seq, n_tensor),
        out_shape=(
            jax.ShapeDtypeStruct((1, experts, tokens, 2 * hidden), jnp.bfloat16),
            jax.ShapeDtypeStruct((1, experts, tokens), jnp.float32),
            jax.ShapeDtypeStruct((experts, hidden, block), jnp.bfloat16),
        ),
        in_specs=[away] * 6,
        out_specs=(whole, whole, whole),
        scratch_shapes=[
            pltpu.SMEM((1, experts), jnp.int32),
            pltpu.VMEM((experts, tokens), jnp.int32),
            pltpu.VMEM((experts, tokens), jnp.float32),
            pltpu.VMEM((n_tensor, halves, tokens, block), jnp.bfloat16),
            pltpu.VMEM((PIECES, n_seq * tokens // PIECES, block), jnp.bfloat16),
            pltpu.VMEM((PIECES, n_seq * tokens // PIECES, experts * hidden), jnp.bfloat16),
            pltpu.VMEM((experts, hidden, width), jnp.bfloat16),
            pltpu.VMEM((experts, tokens, 2 * hidden), jnp.bfloat16),
            pltpu.VMEM((experts, tokens, 2 * hidden), jnp.float32),
            pltpu.VMEM((tokens, experts * hidden), jnp.bfloat16),
            pltpu.VMEM((tokens, experts * hidden), jnp.float32),
            pltpu.VMEM((experts, hidden, block), jnp.float32),
            dma((5 + halves,)),
            dma((2, reach, pieces)),
            dma((2, n_tensor, pieces)),
            dma((n_tensor, pieces)),
            dma((n_tensor, pieces)),
            dma((n_seq, PIECES)),
            dma((n_seq // 2,)),
            dma((n_seq,)),
            dma((n_seq // 2,)),
        ],
        compiler_params=pltpu.CompilerParams(
            collective_id=0, has_side_effects=True, vmem_limit_bytes=40 * 1024 * 1024
        ),
    )(
        *[
            pltpu.with_memory_space_constraint(operand, pltpu.HBM)
            for operand in (slot_count, slot_token, gate_prob, out_grad, down_weight, pre_act)
        ]
    )


def solution(mesh):
    placed = (
        P("seq", "tensor"),
        P("tensor", None, None),
        P("seq", "tensor", None, None),
        P("seq", "tensor", None),
        P("seq", "tensor", None),
        P("seq", "tensor"),
    )
    return jax.shard_map(
        functools.partial(per_device, mesh.shape["seq"], mesh.shape["tensor"]),
        mesh=mesh,
        in_specs=placed,
        out_specs=(
            P("seq", "tensor", None, None),
            P("seq", "tensor", None),
            P("tensor", None, "seq"),
        ),
        check_vma=False,
    )
```
